32 devices in a mesh: groups: 2 (over y), lon: 4 (over z), lat: 2 (over x), feat: 2 (over core).
Axes of the slice: x: 2, y: 2, z: 4, core: 2. Of those that a mesh axis runs over, the one named last changes fastest.
Arguments:
- pix_feat: float32 [4, 4, 64, 2048], P(('groups', 'lat'), 'lon', None, 'feat'), parts along dimension 0, may hold values from -4 to 4
- labels: int32 [4, 4, 2048], P(('groups', 'lat'), 'lon', 'feat'), parts along dimension 0, may hold values from 0 to 11
- lm_feat: float32 [4, 4, 64, 512], P(('groups', 'lat'), 'lon', None, 'feat'), parts along dimension 0, may hold values from -4 to 4
- coefs: float32 [4, 4, 12, 512], P(('groups', 'lat'), 'lon', None, 'feat'), parts along dimension 0, may hold values from -3 to 3
- direction: float32 [4, 4, 12, 512], P(('groups', 'lat'), 'lon', None, 'feat'), parts along dimension 0, may hold values from -3 to 3
- pair_pix: int32 [4, 4, 512], P(('groups', 'lat'), 'lon', 'feat'), parts along dimension 0, may hold values from 0 to 7
- pair_lm: int32 [4, 4, 512], P(('groups', 'lat'), 'lon', 'feat'), parts along dimension 0, may hold values from 0 to 35, as said below
- pair_count: int32 [4, 4, 2], P(('groups', 'lat'), 'lon', 'feat'), parts along dimension 0, may hold values from 4 to 256, as said below
Outputs:
- gradient: float32 [4, 4, 12, 512], P(('groups', 'lat'), 'lon', None, 'feat'), parts along dimension 0
- hess_vec: float32 [4, 4, 12, 512], P(('groups', 'lat'), 'lon', None, 'feat'), parts along dimension 0
The draws below stay inside these ranges and needn't reach their ends.
There are 2 independent parts, one for each index of `groups`. The reference program is written for one: setup_inputs(seed, part) draws one part's arguments, and reference() takes and returns one part's arrays. A program takes and returns all parts, laid end to end along the dimension named above; each array names one. Nothing has to cross between parts.
Inputs may be any that keep to these rules, and one draw needn't show every extreme that they name: `pair_count`: slots at or past their half tile's count hold valid entries that are ignored. `pair_lm`: no block of band 0 names a neighbour in band -1 and no block of band 2 - 1 one in band 2.
All inputs are finite; a program needn't handle non-finite values.
Results may differ from the reference program's by a relative error of at most 0.0003.
Values sent between devices are 32-bit elements; how exact they have to be, the bound alone decides.
A program may use at most 64 MiB of HBM per device.

```python
import math
import jax
import jax.numpy as jnp
from jax import lax

FEATS = 64
CLASSES = 12
BLOCK = 128
PIX_DEV = 1024
PAIRS_DEV = 256
LATS = 2
LONS = 4
HALVES = 2
TILE_LM = 512
TILE_PIX = 2048
PAIRS_TILE = 512
PIX_BLOCKS = 8
NEAR_BLOCKS = 36


def embedding_rows(key, width):
    key_list = jax.random.split(key, 2)
    shape = (LATS, LONS, FEATS, width)
    row_scale = jnp.exp(jax.random.uniform(key_list[0], (LATS, LONS, 1, width), jnp.float32, math.log(0.2), math.log(0.9)))
    noise = jax.random.normal(key_list[1], shape, jnp.float32)
    return noise * row_scale


def draw_pix_feat(key, part):
    key = jax.random.fold_in(key, 13)
    values = embedding_rows(key, TILE_PIX)
    return jnp.clip(values, -4.0, 4.0)


def draw_lm_feat(key, part):
    key = jax.random.fold_in(key, 17)
    values = embedding_rows(key, TILE_LM)
    return jnp.clip(values, -4.0, 4.0)


def draw_coefs(key, part):
    key = jax.random.fold_in(key, 11)
    noise = jax.random.normal(key, (LATS, LONS, CLASSES, TILE_LM), jnp.float32)
    return jnp.clip(noise * 0.5, -2.5, 2.5)


def draw_pair_lm(key, part):
    key = jax.random.fold_in(key, 5)
    key_list = jax.random.split(key, 5)
    shape = (LATS, LONS, PAIRS_TILE)
    lat_middle = jax.random.randint(key_list[0], shape, 0, 3)
    lat_lowest = jax.random.randint(key_list[1], shape, 1, 3)
    lat_highest = jax.random.randint(key_list[2], shape, 0, 2)
    band = jnp.arange(LATS)[:, None, None]
    lat_offset = jnp.where(band == 0, lat_lowest, jnp.where(band == LATS - 1, lat_highest, lat_middle))
    lon_offset = jax.random.randint(key_list[3], shape, 0, 3)
    inner = jax.random.randint(key_list[4], shape, 0, TILE_LM // BLOCK)
    return ((lat_offset * 3 + lon_offset) * (TILE_LM // BLOCK) + inner).astype(jnp.int32)


def draw_pair_count(key, part):
    key = jax.random.fold_in(key, 7)
    key_list = jax.random.split(key, 2)
    level = jax.random.randint(key_list[0], (LATS * LONS * HALVES,), 1, 9)
    counts = jnp.maximum(PAIRS_DEV * level * level // 64, 1)
    busiest = jax.random.randint(key_list[1], (), 0, LATS * LONS * HALVES)
    counts = counts.at[busiest].set(PAIRS_DEV)
    return counts.reshape(LATS, LONS, HALVES).astype(jnp.int32)


def set_ends(entries, stream_key, smallest, top_value):
    extent = entries.shape
    index_at = [jax.random.randint(jax.random.fold_in(stream_key, axis), (), 0, extent[axis]) for axis in range(len(extent))]
    entries = entries.at[tuple(index_at)].set(smallest)
    longest = extent.index(max(extent))
    index_at[longest] = (index_at[longest] + 1) % extent[longest]
    return entries.at[tuple(index_at)].set(top_value)


def block_levels(key, dims, shards, least, high):
    gain, own = 1.0, jax.random.fold_in(key, 6)
    for axis_at, shards_of in shards:
        draws = jnp.exp(jax.random.uniform(jax.random.fold_in(own, axis_at), (shards_of,), jnp.float32, least / len(shards), high / len(shards)))
        gain = gain * jnp.repeat(draws, dims[axis_at] // shards_of).reshape([-1 if axis == axis_at else 1 for axis in range(len(dims))])
    return gain


def centred(own_key, extent, scale, limit, cuts=(), kind=jnp.bfloat16):
    gain = block_levels(own_key, extent, cuts, -0.22, 0.18) if cuts else 1.0
    entries = jax.random.normal(own_key, extent, jnp.float32) * scale * gain
    return jnp.minimum(jnp.maximum(entries, -limit), limit).astype(kind)


def setup_inputs(seed: int = 0, part: int = 0) -> dict:
    key_of = jax.random.split(jax.random.key(seed), 9)
    part_keys = jax.random.split(jax.random.fold_in(key_of[8], part), 9)
    pix_feat = draw_pix_feat(jax.random.fold_in(jax.random.fold_in(key_of[8], part), 71), part)
    labels = set_ends(jax.random.randint(part_keys[1], (LATS, LONS, TILE_PIX), 0, CLASSES), jax.random.fold_in(part_keys[1], 1), 0, CLASSES - 1).astype(jnp.int32)
    lm_feat = draw_lm_feat(jax.random.fold_in(jax.random.fold_in(key_of[8], part), 71), part)
    coefs = draw_coefs(jax.random.fold_in(jax.random.fold_in(key_of[8], part), 71), part)
    direction = centred(part_keys[4], (LATS, LONS, CLASSES, TILE_LM), 0.5, 3.0, ((0, 2), (1, 4), (3, 2)), jnp.float32)
    pair_pix = set_ends(jax.random.randint(part_keys[5], (LATS, LONS, PAIRS_TILE), 0, PIX_BLOCKS), jax.random.fold_in(part_keys[5], 1), 0, PIX_BLOCKS - 1).astype(jnp.int32)
    pair_lm = draw_pair_lm(jax.random.fold_in(jax.random.fold_in(key_of[8], part), 71), part)
    pair_count = draw_pair_count(jax.random.fold_in(jax.random.fold_in(key_of[8], part), 71), part)
    return {"pix_feat": pix_feat, "labels": labels, "lm_feat": lm_feat, "coefs": coefs, "direction": direction, "pair_pix": pair_pix, "pair_lm": pair_lm, "pair_count": pair_count}


kernel_radius = 5.0

def wendland(pix_blocks, pix_sq, lm_blocks, lm_sq, slot_pixel, slot_landmark, live_mask):
    pix_rows = pix_blocks[slot_pixel]
    lm_rows = lm_blocks[slot_landmark]
    cross = jnp.einsum('gfp,gfl->gpl', pix_rows, lm_rows, precision=lax.Precision.HIGHEST)
    distance = pix_sq[slot_pixel][:, :, None] + lm_sq[slot_landmark][:, None, :] - 2.0 * cross
    scaled = jnp.sqrt(distance) / kernel_radius
    remain = jnp.maximum(1.0 - scaled, 0.0)
    squared = remain * remain
    return squared * squared * (4.0 * scaled + 1.0) * live_mask[:, None, None]

def device_terms(pixels, pix_labels, near, slot_pixel, slot_landmark, count):
    lm_blocks_tile = TILE_LM // BLOCK
    stacked = near.reshape(3, 3, FEATS + 2 * CLASSES, lm_blocks_tile, BLOCK)
    stacked = stacked.transpose(0, 1, 3, 2, 4).reshape(NEAR_BLOCKS, FEATS + 2 * CLASSES, BLOCK)
    lm_blocks = stacked[:, :FEATS]
    coefficient_tiles = stacked[:, FEATS:]
    lm_sq = lax.optimization_barrier(jnp.sum(lm_blocks * lm_blocks, axis=1))
    pix_blocks = pixels.reshape(FEATS, PIX_BLOCKS, BLOCK).transpose(1, 0, 2)
    pix_sq = lax.optimization_barrier(jnp.sum(pix_blocks * pix_blocks, axis=1))
    live_mask = (jnp.arange(PAIRS_DEV, dtype=jnp.int32) < count).astype(jnp.float32)
    kernel_weight = wendland(pix_blocks, pix_sq, lm_blocks, lm_sq, slot_pixel, slot_landmark, live_mask)
    contribution = jnp.einsum('vjz,vhz->vjh', coefficient_tiles[slot_landmark], kernel_weight, precision=lax.Precision.HIGHEST)
    forward = jax.ops.segment_sum(contribution, slot_pixel, num_segments=PIX_BLOCKS)
    logits = forward[:, :CLASSES]
    probe = forward[:, CLASSES:]
    highest = lax.optimization_barrier(jnp.max(logits, axis=1, keepdims=True))
    powered = jnp.exp(logits - highest)
    chances = powered / lax.optimization_barrier(jnp.sum(powered, axis=1, keepdims=True))
    label_blocks = pix_labels.reshape(PIX_BLOCKS, BLOCK)
    target = (label_blocks[:, None, :] == jnp.arange(CLASSES, dtype=jnp.int32)[None, :, None]).astype(jnp.float32)
    resid = chances - target
    curv = chances * probe - chances * lax.optimization_barrier(jnp.sum(chances * probe, axis=1, keepdims=True))
    reverse_sweep = jnp.concatenate([resid, curv], axis=1)
    partial_pieces = jnp.einsum('sjr,sru->sju', reverse_sweep[slot_pixel], kernel_weight, precision=lax.Precision.HIGHEST)
    landed = jax.ops.segment_sum(partial_pieces, slot_landmark, num_segments=NEAR_BLOCKS)
    landed = landed.reshape(3, 3, lm_blocks_tile, 2 * CLASSES, BLOCK).transpose(0, 1, 3, 2, 4)
    return landed.reshape(3, 3, 2 * CLASSES, TILE_LM)

def reference(pix_feat, labels, lm_feat, coefs, direction, pair_pix, pair_lm, pair_count):
    landmark_data = jnp.concatenate([lm_feat, coefs, direction], axis=2)
    padded = jnp.pad(landmark_data, ((1, 1), (0, 0), (0, 0), (0, 0)))
    devices_all = LATS * LONS * HALVES

    def one_device(index):
        band = index // (LONS * HALVES)
        column = index // HALVES % LONS
        half_index = index % HALVES
        rows = lax.dynamic_slice_in_dim(padded, band, 3, 0)
        beside_all = (column + jnp.arange(3, dtype=jnp.int32) - 1) % LONS
        near = jnp.take(rows, beside_all, axis=1)
        pixels = lax.dynamic_slice_in_dim(pix_feat[band, column], half_index * PIX_DEV, PIX_DEV, 1)
        pix_labels = lax.dynamic_slice_in_dim(labels[band, column], half_index * PIX_DEV, PIX_DEV, 0)
        slot_pixel = lax.dynamic_slice_in_dim(pair_pix[band, column], half_index * PAIRS_DEV, PAIRS_DEV, 0)
        slot_landmark = lax.dynamic_slice_in_dim(pair_lm[band, column], half_index * PAIRS_DEV, PAIRS_DEV, 0)
        count = pair_count[band, column, half_index]
        return device_terms(pixels, pix_labels, near, slot_pixel, slot_landmark, count)
    indices = jnp.arange(devices_all, dtype=jnp.int32)
    partials = lax.map(one_device, indices)
    band_of = indices // (LONS * HALVES)
    column_of = indices // HALVES % LONS
    offsets = jnp.arange(3, dtype=jnp.int32)
    band_index = band_of[:, None, None] + offsets[None, :, None] + 0 * offsets[None, None, :]
    column_index = (column_of[:, None, None] + offsets[None, None, :] - 1 + 0 * offsets[None, :, None]) % LONS
    total = jnp.zeros((LATS + 2, LONS, 2 * CLASSES, TILE_LM), jnp.float32)
    total = total.at[band_index, column_index].add(partials)
    inside = total[1:-1]
    return (inside[:, :, :CLASSES], inside[:, :, CLASSES:])
```

```python
import functools

import jax
import jax.numpy as jnp
from jax import lax
from jax.experimental import pallas as pl
from jax.experimental.pallas import tpu as pltpu
from jax.sharding import PartitionSpec as P

BLOCK = 128
CHUNK = 256
RADIUS = 5.0
BF16 = jnp.bfloat16
F32 = jnp.float32
NN = (((1,), (0,)), ((), ()))
NT = (((1,), (1,)), ((), ()))


def dot(left, right, numbers):
    return lax.dot_general(left, right, numbers, preferred_element_type=F32)


def parts_of(value):
    high = value.astype(BF16).astype(F32)
    return high, value - high


def three_parts(value):
    first, rest = parts_of(value)
    second, third = parts_of(rest)
    return first, second, third


def stacked_pair(value, rows):
    high, low = parts_of(value)
    both = jnp.concatenate([high, low], axis=0).astype(BF16)
    pad = jnp.zeros((rows - value.shape[0], value.shape[1]), F32)
    return both, jnp.concatenate([high, pad], axis=0).astype(BF16)


def kernel(
    lats,
    lons,
    lm_ref,
    co_ref,
    di_ref,
    px_ref,
    lab_ref,
    pp_ref,
    pn_ref,
    cnt_ref,
    grad_ref,
    hess_ref,
    near,
    kern_hi,
    kern_lo,
    pix_rows,
    weight,
    forward,
    back_both,
    back_high,
    mine,
    part_out,
    part_in,
    tot_out,
    tot_in,
    near_send,
    near_recv,
    pass_send,
    part_send,
    part_recv,
    tot_send,
    tot_recv,
):
    feats, half_lm = lm_ref.shape[2:]
    classes = co_ref.shape[2]
    rows = 2 * classes
    pix = px_ref.shape[3]
    depth = pix_rows.shape[1]
    slots = pp_ref.shape[2]
    side = lax.axis_index("feat")
    band = lax.axis_index("lat")
    column = lax.axis_index("lon")
    partner = {"feat": 1 - side}

    def inside(a):
        return jnp.logical_and(band + a >= 1, band + a <= lats)

    def tile_at(a, b):
        return {"lat": band + a - 1, "lon": lax.rem(column + b - 1 + lons, lons)}

    def order(turn):
        return lax.rem(1 + 2 * lax.rem(turn, 3), 3), lax.rem(1 + 2 * (turn // 3), 3)

    around = [(1, 0), (1, 2), (0, 0), (0, 2), (2, 0), (2, 2), (0, 1), (2, 1)]

    def each_around(act):
        for a, b in around:
            if a == 1:
                act(a, b)
            else:
                pl.when(inside(a))(functools.partial(act, a, b))

    barrier = pltpu.get_barrier_semaphore()

    def greet(a, b):
        pl.semaphore_signal(barrier, inc=1, device_id=tile_at(a, b), device_id_type=pl.DeviceIdType.MESH)

    pl.semaphore_signal(barrier, inc=1, device_id=partner, device_id_type=pl.DeviceIdType.MESH)
    each_around(greet)

    own = 8 + side
    near[own, 0:feats, :] = lm_ref[0, 0]
    near[own, feats : feats + classes, :] = co_ref[0, 0]
    near[own, feats + classes : feats + rows, :] = di_ref[0, 0]

    bands = sum(inside(a).astype(jnp.int32) for a in (0, 1, 2))
    pl.semaphore_wait(barrier, 3 * bands)

    def near_copy(a, b):
        there = (2 - a) * 3 + (2 - b)
        return pltpu.make_async_remote_copy(
            src_ref=near.at[own],
            dst_ref=near.at[2 * there + side],
            send_sem=near_send.at[a * 3 + b],
            recv_sem=near_recv.at[2 * there + side],
            device_id=tile_at(a, b),
            device_id_type=pl.DeviceIdType.MESH,
        )

    def pass_copy(slot):
        return pltpu.make_async_remote_copy(
            src_ref=near.at[2 * slot + side],
            dst_ref=near.at[2 * slot + side],
            send_sem=pass_send.at[slot],
            recv_sem=near_recv.at[2 * slot + side],
            device_id=partner,
            device_id_type=pl.DeviceIdType.MESH,
        )

    def arrived(place):
        return pltpu.make_async_remote_copy(
            src_ref=near.at[place],
            dst_ref=near.at[place],
            send_sem=near_send.at[4],
            recv_sem=near_recv.at[place],
            device_id=partner,
            device_id_type=pl.DeviceIdType.MESH,
        )

    pass_copy(4).start()
    each_around(lambda a, b: near_copy(a, b).start())

    pixels = px_ref[0, 0]
    x_high, x_low = parts_of(pixels * (-2.0 / (RADIUS * RADIUS)))
    x1, x2, x3 = three_parts(jnp.sum(pixels * pixels, axis=0, keepdims=True) * (1.0 / (RADIUS * RADIUS)))
    row = lax.broadcasted_iota(jnp.int32, (depth - 3 * feats, pix), 0)
    extra = jnp.where(
        row < 3,
        1.0,
        jnp.where(row == 3, x1, jnp.where(row == 4, x2, jnp.where(row == 5, x3, 0.0))),
    )
    pix_rows[...] = jnp.concatenate([x_high, x_high, x_low, extra], axis=0).T.astype(BF16)

    pix_blocks = pix // BLOCK
    near_blocks = 18 * half_lm // BLOCK
    used = lax.broadcasted_iota(jnp.int32, (1, slots), 1) < cnt_ref[0, 0, 0]
    pix_hot = jnp.where(
        jnp.logical_and(lax.broadcasted_iota(jnp.int32, (pix_blocks, slots), 0) == pp_ref[0], used), 1.0, 0.0
    ).astype(BF16)
    lm_pad = -(-near_blocks // BLOCK) * BLOCK
    lm_hot = jnp.where(lax.broadcasted_iota(jnp.int32, (lm_pad, slots), 0) == pn_ref[0], 1.0, 0.0).astype(BF16)
    counts = dot(pix_hot, lm_hot, NT).astype(BF16)
    width = near_blocks * BLOCK
    spread = jnp.where(
        lax.broadcasted_iota(jnp.int32, (lm_pad, width), 0)
        == lax.broadcasted_iota(jnp.int32, (lm_pad, width), 1) // BLOCK,
        1.0,
        0.0,
    ).astype(BF16)
    wide = dot(counts, spread, NN)
    for place in range(18):
        weight[place] = wide[:, place * half_lm : (place + 1) * half_lm]

    forward[...] = jnp.zeros_like(forward)
    aux_row = lax.broadcasted_iota(jnp.int32, (depth - 3 * feats, half_lm), 0)

    def forward_half(place):
        z = near[place, 0:feats, :]
        z_high, z_low = parts_of(z)
        z1, z2, z3 = three_parts(jnp.sum(z * z, axis=0, keepdims=True) * (1.0 / (RADIUS * RADIUS)))
        extra = jnp.where(
            aux_row == 0,
            z1,
            jnp.where(aux_row == 1, z2, jnp.where(aux_row == 2, z3, jnp.where(aux_row < 6, 1.0, 0.0))),
        )
        columns = jnp.concatenate([z_high, z_low, z_high, extra], axis=0).astype(BF16)
        both, high = stacked_pair(near[place, feats : feats + rows, :], 32)
        for chunk in range(pix // CHUNK):
            at = slice(chunk * CHUNK, (chunk + 1) * CHUNK)
            dist = jnp.maximum(dot(pix_rows[at, :], columns, NN), 1e-30)
            remain = jnp.maximum(1.0 - dist * lax.rsqrt(dist), 0.0)
            first = chunk * (CHUNK // BLOCK)
            times = jnp.concatenate(
                [
                    jnp.broadcast_to(weight[place, q : q + 1, :], (BLOCK, half_lm))
                    for q in range(first, first + CHUNK // BLOCK)
                ],
                axis=0,
            )
            squared = remain * remain
            value = squared * squared * (5.0 * times - (4.0 * times) * remain)
            value_high = value.astype(BF16)
            value_low = (value - value_high.astype(F32)).astype(BF16)
            kern_hi[place, at, :] = value_high
            kern_lo[place, at, :] = value_low
            upper = dot(both, value_high, NT)
            lower = dot(high, value_low, NT)
            forward[:, at] += upper[:rows] + upper[rows:] + lower[:rows]

    def forward_tile(turn, carry):
        a, b = order(turn)
        slot = a * 3 + b

        @pl.when(inside(a))
        def _():
            @pl.when(turn > 0)
            def _():
                arrived(2 * slot + side).wait_recv()
                pass_copy(slot).start()

            forward_half(2 * slot + side)
            arrived(2 * slot + 1 - side).wait_recv()
            forward_half(2 * slot + 1 - side)

        return carry

    lax.fori_loop(0, 9, forward_tile, 0)

    logits = forward[0:classes, :]
    probe = forward[classes:rows, :]
    powered = jnp.exp(logits - jnp.max(logits, axis=0, keepdims=True))
    chances = powered / jnp.sum(powered, axis=0, keepdims=True)
    target = jnp.where(lax.broadcasted_iota(jnp.int32, (classes, pix), 0) == lab_ref[0], 1.0, 0.0)
    moved = chances * probe
    curv = moved - chances * jnp.sum(moved, axis=0, keepdims=True)
    both, high = stacked_pair(jnp.concatenate([chances - target, curv], axis=0), 32)
    back_both[...] = both
    back_high[...] = high

    def part_copy(slot):
        return pltpu.make_async_remote_copy(
            src_ref=part_out.at[slot],
            dst_ref=part_in.at[slot],
            send_sem=part_send.at[slot],
            recv_sem=part_recv.at[slot],
            device_id=partner,
            device_id_type=pl.DeviceIdType.MESH,
        )

    def tot_copy(a, b):
        slot = a * 3 + b
        return pltpu.make_async_remote_copy(
            src_ref=tot_out.at[slot],
            dst_ref=tot_in.at[8 - slot],
            send_sem=tot_send.at[slot],
            recv_sem=tot_recv.at[8 - slot],
            device_id=tile_at(a, b),
            device_id_type=pl.DeviceIdType.MESH,
        )

    def backward_half(place):
        upper = dot(back_both[...], kern_hi[place], NN)
        lower = dot(back_high[...], kern_lo[place], NN)
        return upper[:rows] + upper[rows:] + lower[:rows]

    def backward_tile(turn, carry):
        a, b = order(8 - turn)
        slot = a * 3 + b

        @pl.when(inside(a))
        def _():
            part_out[slot] = backward_half(2 * slot + 1 - side)
            part_copy(slot).start()
            mine[slot] = backward_half(2 * slot + side)

        a_before, b_before = order(9 - turn)
        before = a_before * 3 + b_before

        @pl.when(jnp.logical_and(turn > 0, inside(a_before)))
        def _():
            part_copy(before).wait_recv()
            tot_out[before] = mine[before] + part_in[before]
            tot_copy(a_before, b_before).start()

        return carry

    lax.fori_loop(0, 9, backward_tile, 0)
    part_copy(4).wait_recv()
    tot_out[4] = mine[4] + part_in[4]

    def take(a, b):
        slot = a * 3 + b
        tot_copy(2 - a, 2 - b).wait_recv()
        tot_out[4] += tot_in[slot]

    each_around(take)
    total = tot_out[4]
    grad_ref[0, 0] = total[:classes]
    hess_ref[0, 0] = total[classes:]

    pass_copy(4).wait_send()
    part_copy(4).wait_send()

    def drain(a, b):
        near_copy(a, b).wait_send()
        pass_copy(a * 3 + b).wait_send()
        part_copy(a * 3 + b).wait_send()
        tot_copy(a, b).wait_send()

    each_around(drain)


def solution(mesh):
    lats, lons = mesh.shape["lat"], mesh.shape["lon"]

    def body(pix_feat, labels, lm_feat, coefs, direction, pair_pix, pair_lm, pair_count):
        feats, half_lm = lm_feat.shape[2:]
        rows = 2 * coefs.shape[2]
        pix = pix_feat.shape[3]
        depth = 4 * feats
        vmem = pl.BlockSpec(memory_space=pltpu.VMEM)
        out = jax.ShapeDtypeStruct(coefs.shape, F32)
        partial = pltpu.VMEM((9, rows, half_lm), F32)
        nine = pltpu.SemaphoreType.DMA((9,))
        return pl.pallas_call(
            functools.partial(kernel, lats, lons),
            out_shape=(out, out),
            in_specs=[vmem] * 7 + [pl.BlockSpec(memory_space=pltpu.SMEM)],
            out_specs=(vmem, vmem),
            scratch_shapes=[
                pltpu.VMEM((18, feats + rows, half_lm), F32),
                pltpu.VMEM((18, pix, half_lm), BF16),
                pltpu.VMEM((18, pix, half_lm), BF16),
                pltpu.VMEM((pix, depth), BF16),
                pltpu.VMEM((18, pix // BLOCK, half_lm), F32),
                pltpu.VMEM((rows, pix), F32),
                pltpu.VMEM((2 * rows, pix), BF16),
                pltpu.VMEM((32, pix), BF16),
                partial,
                partial,
                partial,
                partial,
                partial,
                nine,
                pltpu.SemaphoreType.DMA((18,)),
                nine,
                nine,
                nine,
                nine,
                nine,
            ],
            compiler_params=pltpu.CompilerParams(
                collective_id=0, has_side_effects=True, vmem_limit_bytes=48 * 1024 * 1024
            ),
        )(lm_feat, coefs, direction, pix_feat, labels, pair_pix, pair_lm, pair_count)

    wide = P(("groups", "lat"), "lon", None, "feat")
    flat = P(("groups", "lat"), "lon", "feat")
    return jax.shard_map(
        body,
        mesh=mesh,
        in_specs=(wide, flat, wide, wide, wide, flat, flat, flat),
        out_specs=(wide, wide),
        check_vma=False,
    )
```

```python
import functools

import jax
import jax.numpy as jnp
from jax import lax
from jax.experimental import pallas as pl
from jax.experimental.pallas import tpu as pltpu
from jax.sharding import PartitionSpec as P

BLOCK = 128
CHUNK = 512
RADIUS = 5.0
BF16 = jnp.bfloat16
F32 = jnp.float32
NN = (((1,), (0,)), ((), ()))
NT = (((1,), (1,)), ((), ()))


def dot(left, right, numbers):
    return lax.dot_general(left, right, numbers, preferred_element_type=F32)


def parts_of(value):
    high = value.astype(BF16).astype(F32)
    return high, value - high


def three_parts(value):
    first, rest = parts_of(value)
    second, third = parts_of(rest)
    return first, second, third


def stacked_pair(value, rows):
    high, low = parts_of(value)
    both = jnp.concatenate([high, low], axis=0).astype(BF16)
    pad = jnp.zeros((rows - value.shape[0], value.shape[1]), F32)
    return both, jnp.concatenate([high, pad], axis=0).astype(BF16)


def kernel(
    lats,
    lons,
    lm_hbm,
    co_hbm,
    di_hbm,
    px_hbm,
    lab_hbm,
    pp_hbm,
    pn_hbm,
    cnt_ref,
    grad_ref,
    hess_ref,
    lm_ref,
    co_ref,
    di_ref,
    px_ref,
    lab_ref,
    pp_ref,
    pn_ref,
    load_sem,
    near,
    kern_hi,
    kern_lo,
    pix_rows,
    weight,
    forward,
    back_both,
    back_high,
    part_out,
    part_in,
    tot_out,
    tot_in,
    near_send,
    near_recv,
    pass_send,
    part_send,
    part_recv,
    tot_send,
    tot_recv,
):
    feats, half_lm = lm_ref.shape
    classes = co_ref.shape[0]
    rows = 2 * classes
    pix = px_ref.shape[1]
    depth = pix_rows.shape[1]
    slots = pp_ref.shape[1]
    side = lax.axis_index("feat")
    band = lax.axis_index("lat")
    column = lax.axis_index("lon")
    partner = {"feat": 1 - side}

    def inside(a):
        return jnp.logical_and(band + a >= 1, band + a <= lats)

    def tile_at(a, b):
        return {"lat": band + a - 1, "lon": lax.rem(column + b - 1 + lons, lons)}

    def order(turn):
        return lax.rem(1 + 2 * lax.rem(turn, 3), 3), lax.rem(1 + 2 * (turn // 3), 3)

    around = [(1, 0), (1, 2), (0, 0), (0, 2), (2, 0), (2, 2), (0, 1), (2, 1)]

    def each_around(act):
        for a, b in around:
            if a == 1:
                act(a, b)
            else:
                pl.when(inside(a))(functools.partial(act, a, b))

    loads = [
        pltpu.make_async_copy(source, target, load_sem.at[n])
        for n, (source, target) in enumerate(
            [
                (lm_hbm.at[0, 0], lm_ref),
                (co_hbm.at[0], co_ref),
                (di_hbm.at[0], di_ref),
                (px_hbm.at[0, 0], px_ref),
                (pp_hbm.at[0], pp_ref),
                (pn_hbm.at[0], pn_ref),
                (lab_hbm.at[0], lab_ref),
            ]
        )
    ]
    for load in loads:
        load.start()

    barrier = pltpu.get_barrier_semaphore()

    def greet(a, b):
        pl.semaphore_signal(barrier, inc=1, device_id=tile_at(a, b), device_id_type=pl.DeviceIdType.MESH)

    pl.semaphore_signal(barrier, inc=1, device_id=partner, device_id_type=pl.DeviceIdType.MESH)
    each_around(greet)

    own = 8 + side
    for load in loads[:3]:
        load.wait()
    near[own, 0:feats, :] = lm_ref[...]
    near[own, feats : feats + classes, :] = co_ref[:, 0, :]
    near[own, feats + classes : feats + rows, :] = di_ref[:, 0, :]

    bands = sum(inside(a).astype(jnp.int32) for a in (0, 1, 2))
    pl.semaphore_wait(barrier, 3 * bands)

    def near_copy(a, b):
        there = (2 - a) * 3 + (2 - b)
        return pltpu.make_async_remote_copy(
            src_ref=near.at[own],
            dst_ref=near.at[2 * there + side],
            send_sem=near_send.at[a * 3 + b],
            recv_sem=near_recv.at[2 * there + side],
            device_id=tile_at(a, b),
            device_id_type=pl.DeviceIdType.MESH,
        )

    def pass_copy(slot):
        return pltpu.make_async_remote_copy(
            src_ref=near.at[2 * slot + side],
            dst_ref=near.at[2 * slot + side],
            send_sem=pass_send.at[slot],
            recv_sem=near_recv.at[2 * slot + side],
            device_id=partner,
            device_id_type=pl.DeviceIdType.MESH,
        )

    def arrived(place):
        return pltpu.make_async_remote_copy(
            src_ref=near.at[place],
            dst_ref=near.at[place],
            send_sem=near_send.at[4],
            recv_sem=near_recv.at[place],
            device_id=partner,
            device_id_type=pl.DeviceIdType.MESH,
        )

    pass_copy(4).start()
    each_around(lambda a, b: near_copy(a, b).start())

    for load in loads[3:]:
        load.wait()
    pixels = px_ref[...]
    x_high, x_low = parts_of(pixels * (-2.0 / (RADIUS * RADIUS)))
    x1, x2, x3 = three_parts(jnp.sum(pixels * pixels, axis=0, keepdims=True) * (1.0 / (RADIUS * RADIUS)))
    row = lax.broadcasted_iota(jnp.int32, (depth - 3 * feats, pix), 0)
    extra = jnp.where(
        row < 3,
        1.0,
        jnp.where(row == 3, x1, jnp.where(row == 4, x2, jnp.where(row == 5, x3, 0.0))),
    )
    pix_rows[...] = jnp.concatenate([x_high, x_high, x_low, extra], axis=0).T.astype(BF16)

    pix_blocks = pix // BLOCK
    near_blocks = 18 * half_lm // BLOCK
    used = lax.broadcasted_iota(jnp.int32, (1, slots), 1) < cnt_ref[0, 0, 0]
    pix_hot = jnp.where(
        jnp.logical_and(lax.broadcasted_iota(jnp.int32, (pix_blocks, slots), 0) == pp_ref[...], used), 1.0, 0.0
    ).astype(BF16)
    lm_pad = -(-near_blocks // BLOCK) * BLOCK
    lm_hot = jnp.where(lax.broadcasted_iota(jnp.int32, (lm_pad, slots), 0) == pn_ref[...], 1.0, 0.0).astype(BF16)
    counts = dot(pix_hot, lm_hot, NT).astype(BF16)
    width = near_blocks * BLOCK
    spread = jnp.where(
        lax.broadcasted_iota(jnp.int32, (lm_pad, width), 0)
        == lax.broadcasted_iota(jnp.int32, (lm_pad, width), 1) // BLOCK,
        1.0,
        0.0,
    ).astype(BF16)
    wide = dot(counts, spread, NN)
    for place in range(18):
        weight[place] = wide[:, place * half_lm : (place + 1) * half_lm]

    forward[...] = jnp.zeros_like(forward)
    aux_row = lax.broadcasted_iota(jnp.int32, (depth - 3 * feats, half_lm), 0)

    def forward_half(place):
        z = near[place, 0:feats, :]
        z_high, z_low = parts_of(z)
        z1, z2, z3 = three_parts(jnp.sum(z * z, axis=0, keepdims=True) * (1.0 / (RADIUS * RADIUS)))
        extra = jnp.where(
            aux_row == 0,
            z1,
            jnp.where(aux_row == 1, z2, jnp.where(aux_row == 2, z3, jnp.where(aux_row < 6, 1.0, 0.0))),
        )
        columns = jnp.concatenate([z_high, z_low, z_high, extra], axis=0).astype(BF16)
        both, high = stacked_pair(near[place, feats : feats + rows, :], 32)
        for chunk in range(pix // CHUNK):
            at = slice(chunk * CHUNK, (chunk + 1) * CHUNK)
            dist = jnp.maximum(dot(pix_rows[at, :], columns, NN), 1e-30)
            remain = jnp.maximum(1.0 - dist * lax.rsqrt(dist), 0.0)
            first = chunk * (CHUNK // BLOCK)
            times = jnp.concatenate(
                [
                    jnp.broadcast_to(weight[place, q : q + 1, :], (BLOCK, half_lm))
                    for q in range(first, first + CHUNK // BLOCK)
                ],
                axis=0,
            )
            squared = remain * remain
            value = squared * squared * (5.0 * times - (4.0 * times) * remain)
            value_high = value.astype(BF16)
            value_low = (value - value_high.astype(F32)).astype(BF16)
            kern_hi[place, at, :] = value_high
            kern_lo[place, at, :] = value_low
        for chunk in range(pix // CHUNK):
            at = slice(chunk * CHUNK, (chunk + 1) * CHUNK)
            upper = dot(both, kern_hi[place, at, :], NT)
            lower = dot(high, kern_lo[place, at, :], NT)
            forward[:, at] += upper[:rows] + upper[rows:] + lower[:rows]

    def forward_tile(turn, carry):
        a, b = order(turn)
        slot = a * 3 + b

        @pl.when(inside(a))
        def _():
            @pl.when(turn > 0)
            def _():
                arrived(2 * slot + side).wait_recv()
                pass_copy(slot).start()

            forward_half(2 * slot + side)
            arrived(2 * slot + 1 - side).wait_recv()
            forward_half(2 * slot + 1 - side)

        return carry

    lax.fori_loop(0, 9, forward_tile, 0)

    logits = forward[0:classes, :]
    probe = forward[classes:rows, :]
    powered = jnp.exp(logits - jnp.max(logits, axis=0, keepdims=True))
    chances = powered / jnp.sum(powered, axis=0, keepdims=True)
    target = jnp.where(lax.broadcasted_iota(jnp.int32, (classes, pix), 0) == lab_ref[...], 1.0, 0.0)
    moved = chances * probe
    curv = moved - chances * jnp.sum(moved, axis=0, keepdims=True)
    both, high = stacked_pair(jnp.concatenate([chances - target, curv], axis=0), 32)
    back_both[...] = both
    back_high[...] = high

    def part_copy(slot):
        return pltpu.make_async_remote_copy(
            src_ref=part_out.at[slot],
            dst_ref=part_in.at[slot],
            send_sem=part_send.at[slot],
            recv_sem=part_recv.at[slot],
            device_id=partner,
            device_id_type=pl.DeviceIdType.MESH,
        )

    def tot_copy(a, b):
        slot = a * 3 + b
        return pltpu.make_async_remote_copy(
            src_ref=tot_out.at[slot],
            dst_ref=tot_in.at[8 - slot],
            send_sem=tot_send.at[slot],
            recv_sem=tot_recv.at[8 - slot],
            device_id=tile_at(a, b),
            device_id_type=pl.DeviceIdType.MESH,
        )

    def backward_half(place):
        upper = dot(back_both[...], kern_hi[place], NN)
        lower = dot(back_high[...], kern_lo[place], NN)
        return upper[:rows] + upper[rows:] + lower[:rows]

    def backward_other(turn, carry):
        a, b = order(8 - turn)
        slot = a * 3 + b

        @pl.when(inside(a))
        def _():
            part_out[slot] = backward_half(2 * slot + 1 - side)
            part_copy(slot).start()

        return carry

    def backward_own(turn, carry):
        a, b = order(8 - turn)
        slot = a * 3 + b

        @pl.when(inside(a))
        def _():
            value = backward_half(2 * slot + side)
            part_copy(slot).wait_recv()
            tot_out[slot] = value + part_in[slot]

            @pl.when(turn < 8)
            def _():
                tot_copy(a, b).start()

        return carry

    lax.fori_loop(0, 9, backward_other, 0)
    lax.fori_loop(0, 9, backward_own, 0)

    def take(a, b):
        slot = a * 3 + b
        tot_copy(2 - a, 2 - b).wait_recv()
        tot_out[4] += tot_in[slot]

    each_around(take)
    total = tot_out[4]
    grad_ref[0, :, 0, :] = total[:classes]
    hess_ref[0, :, 0, :] = total[classes:]

    pass_copy(4).wait_send()
    part_copy(4).wait_send()

    def drain(a, b):
        near_copy(a, b).wait_send()
        pass_copy(a * 3 + b).wait_send()
        part_copy(a * 3 + b).wait_send()
        tot_copy(a, b).wait_send()

    each_around(drain)


def solution(mesh):
    lats, lons = mesh.shape["lat"], mesh.shape["lon"]

    def body(pix_feat, labels, lm_feat, coefs, direction, pair_pix, pair_lm, pair_count):
        feats, half_lm = lm_feat.shape[2:]
        rows = 2 * coefs.shape[2]
        pix = pix_feat.shape[3]
        depth = 4 * feats
        vmem = pl.BlockSpec(memory_space=pltpu.VMEM)
        classes = coefs.shape[2]
        out = jax.ShapeDtypeStruct((1, classes, 1, half_lm), F32)
        partial = pltpu.VMEM((9, rows, half_lm), F32)
        nine = pltpu.SemaphoreType.DMA((9,))
        flat_class = pltpu.VMEM((classes, 1, half_lm), F32)
        outs = pl.pallas_call(
            functools.partial(kernel, lats, lons),
            out_shape=(out, out),
            in_specs=[pl.BlockSpec(memory_space=pltpu.HBM)] * 7 + [pl.BlockSpec(memory_space=pltpu.SMEM)],
            out_specs=(vmem, vmem),
            scratch_shapes=[
                pltpu.VMEM((feats, half_lm), F32),
                flat_class,
                flat_class,
                pltpu.VMEM((feats, pix), F32),
                pltpu.VMEM((1, pix), jnp.int32),
                pltpu.VMEM((1, pair_pix.shape[2]), jnp.int32),
                pltpu.VMEM((1, pair_pix.shape[2]), jnp.int32),
                pltpu.SemaphoreType.DMA((7,)),
                pltpu.VMEM((18, feats + rows, half_lm), F32),
                pltpu.VMEM((18, pix, half_lm), BF16),
                pltpu.VMEM((18, pix, half_lm), BF16),
                pltpu.VMEM((pix, depth), BF16),
                pltpu.VMEM((18, pix // BLOCK, half_lm), F32),
                pltpu.VMEM((rows, pix), F32),
                pltpu.VMEM((2 * rows, pix), BF16),
                pltpu.VMEM((32, pix), BF16),
                partial,
                partial,
                partial,
                partial,
                nine,
                pltpu.SemaphoreType.DMA((18,)),
                nine,
                nine,
                nine,
                nine,
                nine,
            ],
            compiler_params=pltpu.CompilerParams(
                collective_id=0, has_side_effects=True, vmem_limit_bytes=64 * 1024 * 1024 - 65536
            ),
        )(
            lm_feat,
            coefs.transpose(0, 2, 1, 3),
            direction.transpose(0, 2, 1, 3),
            pix_feat,
            labels,
            pair_pix,
            pair_lm,
            pair_count,
        )
        return tuple(value.transpose(0, 2, 1, 3) for value in outs)

    wide = P(("groups", "lat"), "lon", None, "feat")
    flat = P(("groups", "lat"), "lon", "feat")
    return jax.shard_map(
        body,
        mesh=mesh,
        in_specs=(wide, flat, wide, wide, wide, flat, flat, flat),
        out_specs=(wide, wide),
        check_vma=False,
    )
```

```python
import functools

import jax
import jax.numpy as jnp
from jax import lax
from jax.experimental import pallas as pl
from jax.experimental.pallas import tpu as pltpu
from jax.sharding import PartitionSpec as P

BLOCK = 128
CHUNK = 512
RADIUS = 5.0
BF16 = jnp.bfloat16
F32 = jnp.float32
NN = (((1,), (0,)), ((), ()))
NT = (((1,), (1,)), ((), ()))


def dot(left, right, numbers):
    return lax.dot_general(left, right, numbers, preferred_element_type=F32)


def parts_of(value):
    high = value.astype(BF16).astype(F32)
    return high, value - high


def three_parts(value):
    first, rest = parts_of(value)
    second, third = parts_of(rest)
    return first, second, third


def stacked_pair(value, rows):
    high, low = parts_of(value)
    both = jnp.concatenate([high, low], axis=0).astype(BF16)
    pad = jnp.zeros((rows - value.shape[0], value.shape[1]), F32)
    return both, jnp.concatenate([high, pad], axis=0).astype(BF16)


def kernel(
    lats,
    lons,
    lm_hbm,
    co_hbm,
    di_hbm,
    px_hbm,
    lab_hbm,
    pp_hbm,
    pn_hbm,
    cnt_ref,
    grad_ref,
    hess_ref,
    lm_ref,
    co_ref,
    di_ref,
    px_ref,
    lab_ref,
    pp_ref,
    pn_ref,
    load_sem,
    near,
    kern_hi,
    kern_lo,
    pix_rows,
    weight,
    forward,
    back_both,
    back_high,
    part_out,
    part_in,
    tot_out,
    tot_in,
    near_send,
    near_recv,
    pass_send,
    part_send,
    part_recv,
    tot_send,
    tot_recv,
):
    feats, half_lm = lm_ref.shape
    classes = co_ref.shape[0]
    rows = 2 * classes
    pix = px_ref.shape[1]
    depth = pix_rows.shape[1]
    slots = pp_ref.shape[1]
    side = lax.axis_index("feat")
    band = lax.axis_index("lat")
    column = lax.axis_index("lon")
    partner = {"feat": 1 - side}

    def inside(a):
        return jnp.logical_and(band + a >= 1, band + a <= lats)

    def tile_at(a, b):
        return {"lat": band + a - 1, "lon": lax.rem(column + b - 1 + lons, lons)}

    def order(turn):
        late = (turn // 3 + 1) // 2
        a = lax.rem(1 + 2 * ((1 - late) * turn + late * ((turn + 1) // 2 - 2)), 3)
        return a, 1 - late + late * 2 * lax.rem(turn + 1, 2)

    around = [(1, 0), (1, 2), (0, 0), (0, 2), (2, 0), (2, 2), (0, 1), (2, 1)]

    def each_around(act):
        for a, b in around:
            if a == 1:
                act(a, b)
            else:
                pl.when(inside(a))(functools.partial(act, a, b))

    loads = [
        pltpu.make_async_copy(source, target, load_sem.at[n])
        for n, (source, target) in enumerate(
            [
                (lm_hbm.at[0, 0], lm_ref),
                (co_hbm.at[0], co_ref),
                (di_hbm.at[0], di_ref),
                (px_hbm.at[0, 0], px_ref),
                (pp_hbm.at[0], pp_ref),
                (pn_hbm.at[0], pn_ref),
                (lab_hbm.at[0], lab_ref),
            ]
        )
    ]
    for load in loads:
        load.start()

    barrier = pltpu.get_barrier_semaphore()

    def greet(a, b):
        pl.semaphore_signal(barrier, inc=1, device_id=tile_at(a, b), device_id_type=pl.DeviceIdType.MESH)

    pl.semaphore_signal(barrier, inc=1, device_id=partner, device_id_type=pl.DeviceIdType.MESH)
    each_around(greet)

    own = 8 + side
    for load in loads[:3]:
        load.wait()
    near[own, 0:feats, :] = lm_ref[...]
    near[own, feats : feats + classes, :] = co_ref[:, 0, :]
    near[own, feats + classes : feats + rows, :] = di_ref[:, 0, :]

    bands = sum(inside(a).astype(jnp.int32) for a in (0, 1, 2))
    pl.semaphore_wait(barrier, 3 * bands)

    def near_copy(a, b):
        corner = a != 1 and b != 1
        there = (2 - a) * 3 + (b if corner else 2 - b)
        return pltpu.make_async_remote_copy(
            src_ref=near.at[2 * (3 + b) + side if corner else own],
            dst_ref=near.at[2 * there + side],
            send_sem=near_send.at[a * 3 + b],
            recv_sem=near_recv.at[2 * there + side],
            device_id=tile_at(a, 1 if corner else b),
            device_id_type=pl.DeviceIdType.MESH,
        )

    def pass_copy(slot):
        return pltpu.make_async_remote_copy(
            src_ref=near.at[2 * slot + side],
            dst_ref=near.at[2 * slot + side],
            send_sem=pass_send.at[slot],
            recv_sem=near_recv.at[2 * slot + side],
            device_id=partner,
            device_id_type=pl.DeviceIdType.MESH,
        )

    def arrived(place):
        return pltpu.make_async_remote_copy(
            src_ref=near.at[place],
            dst_ref=near.at[place],
            send_sem=near_send.at[4],
            recv_sem=near_recv.at[place],
            device_id=partner,
            device_id_type=pl.DeviceIdType.MESH,
        )

    pass_copy(4).start()
    def send_own(a, b):
        if a == 1 or b == 1:
            near_copy(a, b).start()

    each_around(send_own)

    def send_row():
        for b in (0, 2):
            arrived(2 * (3 + b) + side).wait_recv()
            for a in (0, 2):

                @pl.when(inside(a))
                def _():
                    near_copy(a, b).start()

            pass_copy(3 + b).start()

    for load in loads[3:]:
        load.wait()
    pixels = px_ref[...]
    x_high, x_low = parts_of(pixels * (-2.0 / (RADIUS * RADIUS)))
    x1, x2, x3 = three_parts(jnp.sum(pixels * pixels, axis=0, keepdims=True) * (1.0 / (RADIUS * RADIUS)))
    row = lax.broadcasted_iota(jnp.int32, (depth - 3 * feats, pix), 0)
    extra = jnp.where(
        row < 3,
        1.0,
        jnp.where(row == 3, x1, jnp.where(row == 4, x2, jnp.where(row == 5, x3, 0.0))),
    )
    pix_rows[...] = jnp.concatenate([x_high, x_high, x_low, extra], axis=0).T.astype(BF16)

    pix_blocks = pix // BLOCK
    near_blocks = 18 * half_lm // BLOCK
    used = lax.broadcasted_iota(jnp.int32, (1, slots), 1) < cnt_ref[0, 0, 0]
    pix_hot = jnp.where(
        jnp.logical_and(lax.broadcasted_iota(jnp.int32, (pix_blocks, slots), 0) == pp_ref[...], used), 1.0, 0.0
    ).astype(BF16)
    lm_pad = -(-near_blocks // BLOCK) * BLOCK
    lm_hot = jnp.where(lax.broadcasted_iota(jnp.int32, (lm_pad, slots), 0) == pn_ref[...], 1.0, 0.0).astype(BF16)
    counts = dot(pix_hot, lm_hot, NT).astype(BF16)
    width = near_blocks * BLOCK
    spread = jnp.where(
        lax.broadcasted_iota(jnp.int32, (lm_pad, width), 0)
        == lax.broadcasted_iota(jnp.int32, (lm_pad, width), 1) // BLOCK,
        1.0,
        0.0,
    ).astype(BF16)
    wide = dot(counts, spread, NN)
    for place in range(18):
        weight[place] = wide[:, place * half_lm : (place + 1) * half_lm]

    forward[...] = jnp.zeros_like(forward)
    aux_row = lax.broadcasted_iota(jnp.int32, (depth - 3 * feats, half_lm), 0)

    def forward_half(place):
        z = near[place, 0:feats, :]
        z_high, z_low = parts_of(z)
        z1, z2, z3 = three_parts(jnp.sum(z * z, axis=0, keepdims=True) * (1.0 / (RADIUS * RADIUS)))
        extra = jnp.where(
            aux_row == 0,
            z1,
            jnp.where(aux_row == 1, z2, jnp.where(aux_row == 2, z3, jnp.where(aux_row < 6, 1.0, 0.0))),
        )
        columns = jnp.concatenate([z_high, z_low, z_high, extra], axis=0).astype(BF16)
        both, high = stacked_pair(near[place, feats : feats + rows, :], 32)
        for chunk in range(pix // CHUNK):
            at = slice(chunk * CHUNK, (chunk + 1) * CHUNK)
            dist = jnp.maximum(dot(pix_rows[at, :], columns, NN), 1e-30)
            remain = jnp.maximum(1.0 - dist * lax.rsqrt(dist), 0.0)
            first = chunk * (CHUNK // BLOCK)
            times = jnp.concatenate(
                [
                    jnp.broadcast_to(weight[place, q : q + 1, :], (BLOCK, half_lm))
                    for q in range(first, first + CHUNK // BLOCK)
                ],
                axis=0,
            )
            squared = remain * remain
            value = squared * squared * (5.0 * times - (4.0 * times) * remain)
            value_high = value.astype(BF16)
            value_low = (value - value_high.astype(F32)).astype(BF16)
            kern_hi[place, at, :] = value_high
            kern_lo[place, at, :] = value_low
        for chunk in range(pix // CHUNK):
            at = slice(chunk * CHUNK, (chunk + 1) * CHUNK)
            upper = dot(both, kern_hi[place, at, :], NT)
            lower = dot(high, kern_lo[place, at, :], NT)
            forward[:, at] += upper[:rows] + upper[rows:] + lower[:rows]

    def forward_tile(turn, carry):
        a, b = order(turn)
        slot = a * 3 + b

        @pl.when(inside(a))
        def _():
            @pl.when(turn == 3)
            def _():
                send_row()

            @pl.when(jnp.logical_or(turn * (3 - turn) > 0, turn > 4))
            def _():
                arrived(2 * slot + side).wait_recv()
                pass_copy(slot).start()

            forward_half(2 * slot + side)
            arrived(2 * slot + 1 - side).wait_recv()
            forward_half(2 * slot + 1 - side)

        return carry

    lax.fori_loop(0, 9, forward_tile, 0)

    logits = forward[0:classes, :]
    probe = forward[classes:rows, :]
    powered = jnp.exp(logits - jnp.max(logits, axis=0, keepdims=True))
    chances = powered / jnp.sum(powered, axis=0, keepdims=True)
    target = jnp.where(lax.broadcasted_iota(jnp.int32, (classes, pix), 0) == lab_ref[...], 1.0, 0.0)
    moved = chances * probe
    curv = moved - chances * jnp.sum(moved, axis=0, keepdims=True)
    both, high = stacked_pair(jnp.concatenate([chances - target, curv], axis=0), 32)
    back_both[...] = both
    back_high[...] = high

    def part_copy(slot):
        return pltpu.make_async_remote_copy(
            src_ref=part_out.at[slot],
            dst_ref=part_in.at[slot],
            send_sem=part_send.at[slot],
            recv_sem=part_recv.at[slot],
            device_id=partner,
            device_id_type=pl.DeviceIdType.MESH,
        )

    def tot_copy(a, b):
        slot = a * 3 + b
        return pltpu.make_async_remote_copy(
            src_ref=tot_out.at[slot],
            dst_ref=tot_in.at[8 - slot],
            send_sem=tot_send.at[slot],
            recv_sem=tot_recv.at[8 - slot],
            device_id=tile_at(a, b),
            device_id_type=pl.DeviceIdType.MESH,
        )

    def backward_half(place):
        upper = dot(back_both[...], kern_hi[place], NN)
        lower = dot(back_high[...], kern_lo[place], NN)
        return upper[:rows] + upper[rows:] + lower[:rows]

    def backward_other(turn, carry):
        a, b = order(8 - turn)
        slot = a * 3 + b

        @pl.when(inside(a))
        def _():
            part_out[slot] = backward_half(2 * slot + 1 - side)
            part_copy(slot).start()

        return carry

    def backward_own(turn, carry):
        a, b = order(8 - turn)
        slot = a * 3 + b

        @pl.when(inside(a))
        def _():
            value = backward_half(2 * slot + side)
            part_copy(slot).wait_recv()
            tot_out[slot] = value + part_in[slot]

            @pl.when(turn < 8)
            def _():
                tot_copy(a, b).start()

        return carry

    lax.fori_loop(0, 9, backward_other, 0)
    lax.fori_loop(0, 9, backward_own, 0)

    def take(a, b):
        slot = a * 3 + b
        tot_copy(2 - a, 2 - b).wait_recv()
        tot_out[4] += tot_in[slot]

    each_around(take)
    total = tot_out[4]
    grad_ref[0, :, 0, :] = total[:classes]
    hess_ref[0, :, 0, :] = total[classes:]

    pass_copy(4).wait_send()
    part_copy(4).wait_send()

    def drain(a, b):
        near_copy(a, b).wait_send()
        pass_copy(a * 3 + b).wait_send()
        part_copy(a * 3 + b).wait_send()
        tot_copy(a, b).wait_send()

    each_around(drain)


def solution(mesh):
    lats, lons = mesh.shape["lat"], mesh.shape["lon"]

    def body(pix_feat, labels, lm_feat, coefs, direction, pair_pix, pair_lm, pair_count):
        feats, half_lm = lm_feat.shape[2:]
        rows = 2 * coefs.shape[2]
        pix = pix_feat.shape[3]
        depth = 4 * feats
        vmem = pl.BlockSpec(memory_space=pltpu.VMEM)
        classes = coefs.shape[2]
        out = jax.ShapeDtypeStruct((1, classes, 1, half_lm), F32)
        partial = pltpu.VMEM((9, rows, half_lm), F32)
        nine = pltpu.SemaphoreType.DMA((9,))
        flat_class = pltpu.VMEM((classes, 1, half_lm), F32)
        outs = pl.pallas_call(
            functools.partial(kernel, lats, lons),
            out_shape=(out, out),
            in_specs=[pl.BlockSpec(memory_space=pltpu.HBM)] * 7 + [pl.BlockSpec(memory_space=pltpu.SMEM)],
            out_specs=(vmem, vmem),
            scratch_shapes=[
                pltpu.VMEM((feats, half_lm), F32),
                flat_class,
                flat_class,
                pltpu.VMEM((feats, pix), F32),
                pltpu.VMEM((1, pix), jnp.int32),
                pltpu.VMEM((1, pair_pix.shape[2]), jnp.int32),
                pltpu.VMEM((1, pair_pix.shape[2]), jnp.int32),
                pltpu.SemaphoreType.DMA((7,)),
                pltpu.VMEM((18, feats + rows, half_lm), F32),
                pltpu.VMEM((18, pix, half_lm), BF16),
                pltpu.VMEM((18, pix, half_lm), BF16),
                pltpu.VMEM((pix, depth), BF16),
                pltpu.VMEM((18, pix // BLOCK, half_lm), F32),
                pltpu.VMEM((rows, pix), F32),
                pltpu.VMEM((2 * rows, pix), BF16),
                pltpu.VMEM((32, pix), BF16),
                partial,
                partial,
                partial,
                partial,
                nine,
                pltpu.SemaphoreType.DMA((18,)),
                nine,
                nine,
                nine,
                nine,
                nine,
            ],
            compiler_params=pltpu.CompilerParams(
                collective_id=0, has_side_effects=True, vmem_limit_bytes=64 * 1024 * 1024 - 65536
            ),
        )(
            lm_feat,
            coefs.transpose(0, 2, 1, 3),
            direction.transpose(0, 2, 1, 3),
            pix_feat,
            labels,
            pair_pix,
            pair_lm,
            pair_count,
        )
        return tuple(value.transpose(0, 2, 1, 3) for value in outs)

    wide = P(("groups", "lat"), "lon", None, "feat")
    flat = P(("groups", "lat"), "lon", "feat")
    return jax.shard_map(
        body,
        mesh=mesh,
        in_specs=(wide, flat, wide, wide, wide, flat, flat, flat),
        out_specs=(wide, wide),
        check_vma=False,
    )
```

```python
import functools

import jax
import jax.numpy as jnp
from jax import lax
from jax.experimental import pallas as pl
from jax.experimental.pallas import tpu as pltpu
from jax.sharding import PartitionSpec as P

BLOCK = 128
CHUNK = 512
RADIUS = 5.0
BF16 = jnp.bfloat16
F32 = jnp.float32
NN = (((1,), (0,)), ((), ()))
NT = (((1,), (1,)), ((), ()))


def dot(left, right, numbers):
    return lax.dot_general(left, right, numbers, preferred_element_type=F32)


def parts_of(value):
    high = value.astype(BF16).astype(F32)
    return high, value - high


def three_parts(value):
    first, rest = parts_of(value)
    second, third = parts_of(rest)
    return first, second, third


def stacked_pair(value, rows):
    high, low = parts_of(value)
    both = jnp.concatenate([high, low], axis=0).astype(BF16)
    pad = jnp.zeros((rows - value.shape[0], value.shape[1]), F32)
    return both, jnp.concatenate([high, pad], axis=0).astype(BF16)


def kernel(
    lats,
    lons,
    lm_hbm,
    co_hbm,
    di_hbm,
    px_hbm,
    lab_hbm,
    pp_hbm,
    pn_hbm,
    cnt_ref,
    grad_ref,
    hess_ref,
    lm_ref,
    co_ref,
    di_ref,
    px_ref,
    lab_ref,
    pp_ref,
    pn_ref,
    load_sem,
    near,
    kern_hi,
    kern_lo,
    pix_rows,
    weight,
    forward,
    back_both,
    back_high,
    part_out,
    part_in,
    tot_out,
    tot_in,
    near_send,
    near_recv,
    pass_send,
    part_send,
    part_recv,
    tot_send,
    tot_recv,
):
    feats, half_lm = lm_ref.shape
    classes = co_ref.shape[0]
    rows = 2 * classes
    pix = px_ref.shape[1]
    depth = pix_rows.shape[1]
    slots = pp_ref.shape[1]
    side = lax.axis_index("feat")
    band = lax.axis_index("lat")
    column = lax.axis_index("lon")
    partner = {"feat": 1 - side}

    def inside(a):
        return jnp.logical_and(band + a >= 1, band + a <= lats)

    def tile_at(a, b):
        return {"lat": band + a - 1, "lon": lax.rem(column + b - 1 + lons, lons)}

    first = 2 * (column == 0).astype(jnp.int32)

    def order(turn):
        late = (turn // 3 + 1) // 2
        a = lax.rem(1 + 2 * ((1 - late) * turn + late * ((turn + 1) // 2 - 2)), 3)
        return a, 1 - late + late * (first + (1 - first) * 2 * lax.rem(turn + 1, 2))

    around = [(1, 0), (1, 2), (0, 0), (0, 2), (2, 0), (2, 2), (0, 1), (2, 1)]

    def each_around(act):
        for a, b in around:
            if a == 1:
                act(a, b)
            else:
                pl.when(inside(a))(functools.partial(act, a, b))

    loads = [
        pltpu.make_async_copy(source, target, load_sem.at[n])
        for n, (source, target) in enumerate(
            [
                (lm_hbm.at[0, 0], lm_ref),
                (co_hbm.at[0], co_ref),
                (di_hbm.at[0], di_ref),
                (px_hbm.at[0, 0], px_ref),
                (pp_hbm.at[0], pp_ref),
                (pn_hbm.at[0], pn_ref),
                (lab_hbm.at[0], lab_ref),
            ]
        )
    ]
    for load in loads:
        load.start()

    barrier = pltpu.get_barrier_semaphore()

    def greet(a, b):
        pl.semaphore_signal(barrier, inc=1, device_id=tile_at(a, b), device_id_type=pl.DeviceIdType.MESH)

    pl.semaphore_signal(barrier, inc=1, device_id=partner, device_id_type=pl.DeviceIdType.MESH)
    each_around(greet)

    own = 8 + side
    for load in loads[:3]:
        load.wait()
    near[own, 0:feats, :] = lm_ref[...]
    near[own, feats : feats + classes, :] = co_ref[:, 0, :]
    near[own, feats + classes : feats + rows, :] = di_ref[:, 0, :]

    bands = sum(inside(a).astype(jnp.int32) for a in (0, 1, 2))
    pl.semaphore_wait(barrier, 3 * bands)

    def near_copy(a, b, corner):
        there = (2 - a) * 3 + (b if corner else 2 - b)
        return pltpu.make_async_remote_copy(
            src_ref=near.at[2 * (3 + b) + side if corner else own],
            dst_ref=near.at[2 * there + side],
            send_sem=near_send.at[a * 3 + b],
            recv_sem=near_recv.at[2 * there + side],
            device_id=tile_at(a, 1 if corner else b),
            device_id_type=pl.DeviceIdType.MESH,
        )

    def pass_copy(slot):
        return pltpu.make_async_remote_copy(
            src_ref=near.at[2 * slot + side],
            dst_ref=near.at[2 * slot + side],
            send_sem=pass_send.at[slot],
            recv_sem=near_recv.at[2 * slot + side],
            device_id=partner,
            device_id_type=pl.DeviceIdType.MESH,
        )

    def arrived(place):
        return pltpu.make_async_remote_copy(
            src_ref=near.at[place],
            dst_ref=near.at[place],
            send_sem=near_send.at[4],
            recv_sem=near_recv.at[place],
            device_id=partner,
            device_id_type=pl.DeviceIdType.MESH,
        )

    pass_copy(4).start()
    def send_own(a, b):
        if a == 1 or b == 1:
            near_copy(a, b, False).start()

    each_around(send_own)

    def relay(b):
        arrived(2 * (3 + b) + side).wait_recv()
        for a in (0, 2):

            @pl.when(inside(a))
            def _():
                near_copy(a, b, True).start()

        pass_copy(3 + b).start()

    for load in loads[3:]:
        load.wait()
    pixels = px_ref[...]
    x_high, x_low = parts_of(pixels * (-2.0 / (RADIUS * RADIUS)))
    x1, x2, x3 = three_parts(jnp.sum(pixels * pixels, axis=0, keepdims=True) * (1.0 / (RADIUS * RADIUS)))
    row = lax.broadcasted_iota(jnp.int32, (depth - 3 * feats, pix), 0)
    extra = jnp.where(
        row < 3,
        1.0,
        jnp.where(row == 3, x1, jnp.where(row == 4, x2, jnp.where(row == 5, x3, 0.0))),
    )
    pix_rows[...] = jnp.concatenate([x_high, x_high, x_low, extra], axis=0).T.astype(BF16)

    pix_blocks = pix // BLOCK
    near_blocks = 18 * half_lm // BLOCK
    used = lax.broadcasted_iota(jnp.int32, (1, slots), 1) < cnt_ref[0, 0, 0]
    pix_hot = jnp.where(
        jnp.logical_and(lax.broadcasted_iota(jnp.int32, (pix_blocks, slots), 0) == pp_ref[...], used), 1.0, 0.0
    ).astype(BF16)
    lm_pad = -(-near_blocks // BLOCK) * BLOCK
    lm_hot = jnp.where(lax.broadcasted_iota(jnp.int32, (lm_pad, slots), 0) == pn_ref[...], 1.0, 0.0).astype(BF16)
    counts = dot(pix_hot, lm_hot, NT).astype(BF16)
    width = near_blocks * BLOCK
    spread = jnp.where(
        lax.broadcasted_iota(jnp.int32, (lm_pad, width), 0)
        == lax.broadcasted_iota(jnp.int32, (lm_pad, width), 1) // BLOCK,
        1.0,
        0.0,
    ).astype(BF16)
    wide = dot(counts, spread, NN)
    for place in range(18):
        weight[place] = wide[:, place * half_lm : (place + 1) * half_lm]

    forward[...] = jnp.zeros_like(forward)
    aux_row = lax.broadcasted_iota(jnp.int32, (depth - 3 * feats, half_lm), 0)

    def forward_half(place):
        z = near[place, 0:feats, :]
        z_high, z_low = parts_of(z)
        z1, z2, z3 = three_parts(jnp.sum(z * z, axis=0, keepdims=True) * (1.0 / (RADIUS * RADIUS)))
        extra = jnp.where(
            aux_row == 0,
            z1,
            jnp.where(aux_row == 1, z2, jnp.where(aux_row == 2, z3, jnp.where(aux_row < 6, 1.0, 0.0))),
        )
        columns = jnp.concatenate([z_high, z_low, z_high, extra], axis=0).astype(BF16)
        both, high = stacked_pair(near[place, feats : feats + rows, :], 32)
        for chunk in range(pix // CHUNK):
            at = slice(chunk * CHUNK, (chunk + 1) * CHUNK)
            dist = jnp.maximum(dot(pix_rows[at, :], columns, NN), 1e-30)
            remain = jnp.maximum(1.0 - dist * lax.rsqrt(dist), 0.0)
            first = chunk * (CHUNK // BLOCK)
            times = jnp.concatenate(
                [
                    jnp.broadcast_to(weight[place, q : q + 1, :], (BLOCK, half_lm))
                    for q in range(first, first + CHUNK // BLOCK)
                ],
                axis=0,
            )
            squared = remain * remain
            value = squared * squared * (5.0 * times - (4.0 * times) * remain)
            value_high = value.astype(BF16)
            value_low = (value - value_high.astype(F32)).astype(BF16)
            kern_hi[place, at, :] = value_high
            kern_lo[place, at, :] = value_low
        for chunk in range(pix // CHUNK):
            at = slice(chunk * CHUNK, (chunk + 1) * CHUNK)
            upper = dot(both, kern_hi[place, at, :], NT)
            lower = dot(high, kern_lo[place, at, :], NT)
            forward[:, at] += upper[:rows] + upper[rows:] + lower[:rows]

    def forward_tile(turn, carry):
        a, b = order(turn)
        slot = a * 3 + b

        @pl.when(inside(a))
        def _():
            @pl.when(turn == 3)
            def _():
                relay(first)

            @pl.when(jnp.logical_or(turn * (3 - turn) > 0, turn > 4))
            def _():
                arrived(2 * slot + side).wait_recv()
                pass_copy(slot).start()

            forward_half(2 * slot + side)

            @pl.when(turn == 3)
            def _():
                relay(2 - first)

            arrived(2 * slot + 1 - side).wait_recv()
            forward_half(2 * slot + 1 - side)

        return carry

    lax.fori_loop(0, 9, forward_tile, 0)

    logits = forward[0:classes, :]
    probe = forward[classes:rows, :]
    powered = jnp.exp(logits - jnp.max(logits, axis=0, keepdims=True))
    chances = powered / jnp.sum(powered, axis=0, keepdims=True)
    target = jnp.where(lax.broadcasted_iota(jnp.int32, (classes, pix), 0) == lab_ref[...], 1.0, 0.0)
    moved = chances * probe
    curv = moved - chances * jnp.sum(moved, axis=0, keepdims=True)
    both, high = stacked_pair(jnp.concatenate([chances - target, curv], axis=0), 32)
    back_both[...] = both
    back_high[...] = high

    def part_copy(slot):
        return pltpu.make_async_remote_copy(
            src_ref=part_out.at[slot],
            dst_ref=part_in.at[slot],
            send_sem=part_send.at[slot],
            recv_sem=part_recv.at[slot],
            device_id=partner,
            device_id_type=pl.DeviceIdType.MESH,
        )

    def tot_copy(a, b):
        slot = a * 3 + b
        return pltpu.make_async_remote_copy(
            src_ref=tot_out.at[slot],
            dst_ref=tot_in.at[8 - slot],
            send_sem=tot_send.at[slot],
            recv_sem=tot_recv.at[8 - slot],
            device_id=tile_at(a, b),
            device_id_type=pl.DeviceIdType.MESH,
        )

    def backward_half(place):
        upper = dot(back_both[...], kern_hi[place], NN)
        lower = dot(back_high[...], kern_lo[place], NN)
        return upper[:rows] + upper[rows:] + lower[:rows]

    def backward_other(turn, carry):
        a, b = order(8 - turn)
        slot = a * 3 + b

        @pl.when(inside(a))
        def _():
            part_out[slot] = backward_half(2 * slot + 1 - side)
            part_copy(slot).start()

        return carry

    def backward_own(turn, carry):
        a, b = order(8 - turn)
        slot = a * 3 + b

        @pl.when(inside(a))
        def _():
            value = backward_half(2 * slot + side)
            part_copy(slot).wait_recv()
            tot_out[slot] = value + part_in[slot]

            @pl.when(turn < 8)
            def _():
                tot_copy(a, b).start()

        return carry

    lax.fori_loop(0, 9, backward_other, 0)
    lax.fori_loop(0, 9, backward_own, 0)

    def take(a, b):
        slot = a * 3 + b
        tot_copy(2 - a, 2 - b).wait_recv()
        tot_out[4] += tot_in[slot]

    each_around(take)
    total = tot_out[4]
    grad_ref[0, :, 0, :] = total[:classes]
    hess_ref[0, :, 0, :] = total[classes:]

    pass_copy(4).wait_send()
    part_copy(4).wait_send()

    def drain(a, b):
        near_copy(a, b, a != 1 and b != 1).wait_send()
        pass_copy(a * 3 + b).wait_send()
        part_copy(a * 3 + b).wait_send()
        tot_copy(a, b).wait_send()

    each_around(drain)


def solution(mesh):
    lats, lons = mesh.shape["lat"], mesh.shape["lon"]

    def body(pix_feat, labels, lm_feat, coefs, direction, pair_pix, pair_lm, pair_count):
        feats, half_lm = lm_feat.shape[2:]
        rows = 2 * coefs.shape[2]
        pix = pix_feat.shape[3]
        depth = 4 * feats
        vmem = pl.BlockSpec(memory_space=pltpu.VMEM)
        classes = coefs.shape[2]
        out = jax.ShapeDtypeStruct((1, classes, 1, half_lm), F32)
        partial = pltpu.VMEM((9, rows, half_lm), F32)
        nine = pltpu.SemaphoreType.DMA((9,))
        flat_class = pltpu.VMEM((classes, 1, half_lm), F32)
        outs = pl.pallas_call(
            functools.partial(kernel, lats, lons),
            out_shape=(out, out),
            in_specs=[pl.BlockSpec(memory_space=pltpu.HBM)] * 7 + [pl.BlockSpec(memory_space=pltpu.SMEM)],
            out_specs=(vmem, vmem),
            scratch_shapes=[
                pltpu.VMEM((feats, half_lm), F32),
                flat_class,
                flat_class,
                pltpu.VMEM((feats, pix), F32),
                pltpu.VMEM((1, pix), jnp.int32),
                pltpu.VMEM((1, pair_pix.shape[2]), jnp.int32),
                pltpu.VMEM((1, pair_pix.shape[2]), jnp.int32),
                pltpu.SemaphoreType.DMA((7,)),
                pltpu.VMEM((18, feats + rows, half_lm), F32),
                pltpu.VMEM((18, pix, half_lm), BF16),
                pltpu.VMEM((18, pix, half_lm), BF16),
                pltpu.VMEM((pix, depth), BF16),
                pltpu.VMEM((18, pix // BLOCK, half_lm), F32),
                pltpu.VMEM((rows, pix), F32),
                pltpu.VMEM((2 * rows, pix), BF16),
                pltpu.VMEM((32, pix), BF16),
                partial,
                partial,
                partial,
                partial,
                nine,
                pltpu.SemaphoreType.DMA((18,)),
                nine,
                nine,
                nine,
                nine,
                nine,
            ],
            compiler_params=pltpu.CompilerParams(
                collective_id=0, has_side_effects=True, vmem_limit_bytes=64 * 1024 * 1024 - 65536
            ),
        )(
            lm_feat,
            coefs.transpose(0, 2, 1, 3),
            direction.transpose(0, 2, 1, 3),
            pix_feat,
            labels,
            pair_pix,
            pair_lm,
            pair_count,
        )
        return tuple(value.transpose(0, 2, 1, 3) for value in outs)

    wide = P(("groups", "lat"), "lon", None, "feat")
    flat = P(("groups", "lat"), "lon", "feat")
    return jax.shard_map(
        body,
        mesh=mesh,
        in_specs=(wide, flat, wide, wide, wide, flat, flat, flat),
        out_specs=(wide, wide),
        check_vma=False,
    )
```
